256 devices in a mesh: row: 32 (over x_lo, z, core), col: 8 (over y, x_hi).
Axes of the slice: x: 4 (x_hi: 2, x_lo: 2; x = x_hi * 2 + x_lo), y: 4, z: 8, core: 2. Of those that a mesh axis runs over, the one named last changes fastest.
Arguments:
- features: bfloat16 [65536, 602], P(('row', 'col')), may hold values from -6 to 6
- weight: bfloat16 [602, 256], replicated, may hold values from -0.25 to 0.25
- adj_tiles: bfloat16 [32, 8, 32, 6, 128, 128], P('row', 'col'), may hold values from 0.00077819824 to 0.03125
- tile_row: int32 [32, 8, 32, 6], P('row', 'col'), may hold values from 0 to 15, as said below
- tile_col: int32 [32, 8, 32, 6], P('row', 'col'), may hold values from 0 to 1
- tile_count: int32 [32, 8, 32], P('row', 'col'), may hold values from 1 to 6, as said below
- train_mask: int32 [65536], P(('row', 'col')), may hold values 0 or 1
- cotangent: bfloat16 [65536, 256], P(('row', 'col')), may hold values from -6 to 6
Outputs:
- hidden: bfloat16 [65536, 256], P(('row', 'col'))
- grad_features: bfloat16 [65536, 602], P(('row', 'col'))
- grad_weight: float32 [602, 256], replicated
The draws below stay inside these ranges and needn't reach their ends.
Inputs may be any that keep to these rules, and one draw needn't show every extreme that they name: For each [r, c, j], the pairs (tile_row, tile_col) of the slots are distinct. tile_count[r, c, r] = 6 for every r and c.
All inputs are finite; a program needn't handle non-finite values. No bound on the sum of `train_mask` on one device may be relied on, other than what follows from the above.
Results may differ from the reference program's by a relative error of at most 0.0075.
Values may be sent and summed in bfloat16 or wider, within the bound.
No kernel may reach another device: no remote copies, remote signals or barrier semaphores. Data moves between devices by JAX's collectives and lax.ppermute only.
A program may use at most 128 MiB of HBM per device.

```python
import math
import jax
import jax.numpy as jnp
from jax import lax

F_IN = 602
HID = 256
TILE = 128
BLOCK_TILES = 2
SLOTS = 6
ROW_TILES = 16
NODES = 65536
N_ROW = 32
N_COL = 8


def tile_positions(key):
    key_list = jax.random.split(key, N_ROW * N_COL * N_ROW)
    shuffled = jax.vmap(lambda one_key: jax.random.permutation(one_key, ROW_TILES * BLOCK_TILES))(key_list)
    return shuffled[:, :SLOTS].reshape(N_ROW, N_COL, N_ROW, SLOTS).astype(jnp.int32)


def draw_tile_row(key, part):
    placed = tile_positions(key)
    return (placed // BLOCK_TILES).astype(jnp.int32)


def draw_tile_col(key, part):
    placed = tile_positions(key)
    return (placed % BLOCK_TILES).astype(jnp.int32)


def draw_tile_count(key, part):
    key = jax.random.fold_in(key, 3)
    first_key, second_key = jax.random.split(key)
    device_limit = jax.random.randint(first_key, (N_ROW, N_COL, 1), (SLOTS + 1) // 2, SLOTS + 1)
    raw_count = jax.random.randint(second_key, (N_ROW, N_COL, N_ROW), 1, SLOTS + 1)
    clipped = jnp.minimum(raw_count, device_limit)
    diagonal = jnp.arange(N_ROW)[:, None, None] == jnp.arange(N_ROW)[None, None, :]
    return jnp.where(diagonal, SLOTS, clipped).astype(jnp.int32)


def place_ends(result, own_key, low, largest):
    longest = result.shape.index(max(result.shape))
    spots = []
    for shift in (0, 1):
        where = [jax.random.randint(jax.random.fold_in(own_key, axis), (), 0, length) for axis, length in enumerate(result.shape)]
        where[longest] = (where[longest] + shift) % result.shape[longest]
        spots.append(tuple(where))
    return result.at[spots[0]].set(low).at[spots[1]].set(largest)


def levels(stream_key, extent, cuts, smallest, high):
    def one(dim, parts):
        heights = jax.random.uniform(jax.random.fold_in(jax.random.fold_in(stream_key, 6), dim), (parts,), jnp.float32, smallest / len(cuts), high / len(cuts))
        return jnp.repeat(jnp.exp(heights), extent[dim] // parts).reshape((-1,) + (1,) * (len(extent) - dim - 1))

    gain = one(*cuts[0])
    for cut in cuts[1:]:
        gain = gain * one(*cut)
    return gain


def normal_values(own_key, dims, width, most, cuts=(), held_as=jnp.bfloat16):
    array = jax.random.normal(own_key, dims, jnp.float32) * width
    if len(cuts) > 0:
        array = levels(own_key, dims, cuts, -0.22, 0.18) * array
    return jnp.clip(array, min=-most, max=most).astype(held_as)


def setup_inputs(seed: int = 0) -> dict:
    streams_of = jax.random.split(jax.random.key(seed), 9)
    return {
        "features": normal_values(streams_of[0], (NODES, F_IN), 1.0, 6.0, ((0, 256),)),
        "weight": normal_values(streams_of[1], (F_IN, HID), F_IN ** -0.5, 0.25),
        "adj_tiles": jnp.clip(0.00077819824 + 0.030471802 * jax.random.uniform(streams_of[2], (N_ROW, N_COL, N_ROW, SLOTS, TILE, TILE), jnp.float32) ** levels(streams_of[2], (N_ROW, N_COL, N_ROW, SLOTS, TILE, TILE), ((0, 32), (1, 8)), -0.2, 0.2), 0.00077819824, 0.03125).astype(jnp.bfloat16),
        "tile_row": draw_tile_row(jax.random.fold_in(streams_of[8], 71), 0),
        "tile_col": draw_tile_col(jax.random.fold_in(streams_of[8], 71), 0),
        "tile_count": draw_tile_count(jax.random.fold_in(streams_of[8], 71), 0),
        "train_mask": place_ends((jax.random.randint(streams_of[6], (NODES,), 0, 3) < 2).astype(jnp.int32), jax.random.fold_in(streams_of[6], 1), 0, 1),
        "cotangent": normal_values(streams_of[7], (NODES, HID), 1.0, 6.0, ((0, 256),)),
    }


def reference(features, weight, adj_tiles, tile_row, tile_col, tile_count, train_mask, cotangent):
    precise = lax.Precision.HIGHEST
    projected = jnp.dot(features, weight, preferred_element_type=jnp.float32).astype(jnp.bfloat16)
    blocks = projected.reshape(N_ROW, N_COL, BLOCK_TILES, TILE, HID)
    live_slots = (jnp.arange(SLOTS, dtype=jnp.int32)[None, None, None, :] < tile_count[..., None]).astype(jnp.float32)
    block_pick = jnp.arange(N_ROW, dtype=jnp.int32)[None, :, None]
    column_pick = jnp.arange(N_COL, dtype=jnp.int32)[:, None, None]
    row_range = jnp.arange(ROW_TILES, dtype=jnp.int32)
    col_range = jnp.arange(BLOCK_TILES, dtype=jnp.int32)

    def forward_row(pieces):
        adj_blocks, row_ids, col_ids, live_here = pieces
        picked = blocks[block_pick, column_pick, col_ids].astype(jnp.float32)
        product = jnp.einsum('cjkab,cjkbh->cjkah', adj_blocks.astype(jnp.float32), picked, precision=precise)
        product = product * live_here[..., None, None]
        row_hot = (row_ids[..., None] == row_range).astype(jnp.float32)
        return jnp.einsum('cjkr,cjkah->rah', row_hot, product, precision=precise)
    pre_act = lax.map(forward_row, (adj_tiles, tile_row, tile_col, live_slots)).reshape(NODES, HID)
    gate_value = jax.nn.sigmoid(pre_act)
    hidden = (pre_act * gate_value).astype(jnp.bfloat16)
    grad_pre = (cotangent.astype(jnp.float32) * train_mask.astype(jnp.float32)[:, None] * gate_value * (1.0 + pre_act * (1.0 - gate_value))).astype(jnp.bfloat16)
    grad_blocks = grad_pre.reshape(N_ROW, ROW_TILES, TILE, HID)

    def backward_row(grad_acc, pieces):
        adj_blocks, row_ids, col_ids, live_here, grad_here = pieces
        picked = grad_here[row_ids].astype(jnp.float32)
        product = jnp.einsum('cjkab,cjkah->cjkbh', adj_blocks.astype(jnp.float32), picked, precision=precise)
        product = product * live_here[..., None, None]
        col_hot = (col_ids[..., None] == col_range).astype(jnp.float32)
        partial_value = jnp.einsum('cjkt,cjkbh->jctbh', col_hot, product, precision=precise)
        return (grad_acc + partial_value.reshape(NODES, HID), None)
    grad_acc, _ = lax.scan(backward_row, jnp.zeros((NODES, HID), jnp.float32), (adj_tiles, tile_row, tile_col, live_slots, grad_blocks))
    grad_proj = grad_acc.astype(jnp.bfloat16)
    grad_weight = lax.dot_general(features, grad_proj, (((0,), (0,)), ((), ())), preferred_element_type=jnp.float32) * (1.0 / math.sqrt(NODES))
    grad_features = lax.dot_general(grad_proj, weight, (((1,), (1,)), ((), ())), preferred_element_type=jnp.float32).astype(jnp.bfloat16)
    return (hidden, grad_features, grad_weight)
```

```python
import functools
import math

import jax
import jax.numpy as jnp
from jax import lax
from jax.experimental import pallas as pl
from jax.experimental.pallas import tpu as pltpu
from jax.sharding import PartitionSpec as P

ROWS, COLS, ZS = 32, 8, 8
BF, F32 = jnp.bfloat16, jnp.float32
VMEM = 60 << 20
WEIGHT_ROWS = 640

CORE = [(i, i ^ 1) for i in range(ROWS)]
XLO = [(i, i ^ 16) for i in range(ROWS)]
XHI = [(i, i ^ 1) for i in range(COLS)]


def ring_z(step):
    return [(i, (i // 16) * 16 + (i % 16 + 2 * step) % 16) for i in range(ROWS)]


def ring_y(step):
    return [(i, (i + 2 * step) % COLS) for i in range(COLS)]


def ring_x(step):
    route = []
    for r in range(ROWS):
        for c in range(COLS):
            x = ((c % 2) * 2 + r // 16 + step) % 4
            route.append((r * COLS + c, ((x % 2) * 16 + r % 16) * COLS + (c // 2) * 2 + x // 2))
    return route


def to_row(value, route):
    return lax.ppermute(value, "row", route)


def to_col(value, route):
    return lax.ppermute(value, "col", route)


def masked_tiles(tiles, cols, first):
    placed = []
    for s in range(tiles.shape[0]):
        tile, where = tiles[s], cols[first + s]
        zero = jnp.zeros_like(tile)
        placed.append(
            jnp.concatenate([jnp.where(where == 0, tile, zero), jnp.where(where == 1, tile, zero)], axis=1)
        )
    return jnp.concatenate(placed, axis=0)


def forward_kernel(half, fresh, last, blocks, rows, cols, adj, *refs):
    pairs, (held, tiles, total, held_sems, tile_sems, total_sem) = refs[:half], refs[-6:]
    outs = refs[half + (0 if fresh else 1) : -6]
    slots = tiles.shape[1]
    for q in range(half):
        pltpu.make_async_copy(pairs[q], held.at[q], held_sems.at[q]).start()
        for k in (2 * q, 2 * q + 1):
            pltpu.make_async_copy(adj.at[blocks[k]], tiles.at[k], tile_sems.at[k]).start()
    if fresh:
        total[...] = jnp.zeros_like(total)
    else:
        carried = pltpu.make_async_copy(refs[half], total, total_sem)
        carried.start()
        carried.wait()

    def step(q, _):
        pltpu.make_async_copy(pairs[0], held.at[q], held_sems.at[q]).wait()
        for k in (2 * q, 2 * q + 1):
            pltpu.make_async_copy(adj.at[0], tiles.at[k], tile_sems.at[k]).wait()
        products = []
        for far in range(2):
            k = 2 * q + far
            lhs = masked_tiles(tiles.at[k], cols, blocks[k] * slots)
            products.append(jnp.dot(lhs, held[q, far], preferred_element_type=F32))
        for far in range(2):
            first = blocks[2 * q + far] * slots
            for s in range(slots):
                total[rows[first + s]] += products[far][s * 128 : (s + 1) * 128]
        return 0

    lax.fori_loop(0, half, step, 0)
    if not last:
        carried = pltpu.make_async_copy(total, outs[0], total_sem)
        carried.start()
        carried.wait()
        return
    outs[0][...] = total[:2].reshape(256, 256)
    for p in range(1, COLS):
        outs[p][...] = total[2 * p : 2 * p + 2].reshape(256, 256).astype(BF)


def forward_part(adj, rows, cols, blocks, pairs, total, last):
    slots, half = adj.shape[1], len(pairs)
    smem, hbm = pl.BlockSpec(memory_space=pltpu.SMEM), pl.BlockSpec(memory_space=pltpu.HBM)
    vmem = pl.BlockSpec(memory_space=pltpu.VMEM)
    operands = list(pairs) + ([] if total is None else [total])
    if last:
        shapes = [jax.ShapeDtypeStruct((256, 256), F32 if p == 0 else BF) for p in range(COLS)]
    else:
        shapes = [jax.ShapeDtypeStruct((16, 128, 256), F32)]
    outs = pl.pallas_call(
        functools.partial(forward_kernel, half, total is None, last),
        in_specs=[smem] * 3 + [hbm] * (1 + len(operands)),
        out_specs=[vmem if last else hbm] * len(shapes),
        out_shape=shapes,
        scratch_shapes=[
            pltpu.VMEM((half, 2, 256, 256), BF),
            pltpu.VMEM((2 * half, slots, 128, 128), BF),
            pltpu.VMEM((16, 128, 256), F32),
            pltpu.SemaphoreType.DMA((half,)),
            pltpu.SemaphoreType.DMA((2 * half,)),
            pltpu.SemaphoreType.DMA,
        ],
        cost_estimate=pl.CostEstimate(
            flops=4 * half * 768 * 256 * 256, bytes_accessed=half * (1 << 20) + (1 << 22), transcendentals=0
        ),
        compiler_params=pltpu.CompilerParams(vmem_limit_bytes=VMEM),
    )(blocks, rows, cols, adj, *operands)
    return outs if last else outs[0]


def backward_kernel(blocks, rows, cols, adj, grads, *refs):
    out, tiles, sems = refs[-3:]
    count, slots = tiles.shape[:2]
    for k in range(count):
        pltpu.make_async_copy(adj.at[blocks[k]], tiles.at[k], sems.at[k]).start()

    def step(q, _):
        for k in (2 * q, 2 * q + 1):
            pltpu.make_async_copy(adj.at[0], tiles.at[k], sems.at[k]).wait()
        for k in (2 * q, 2 * q + 1):
            first = blocks[k] * slots
            rhs = masked_tiles(tiles.at[k], cols, first)
            lhs = jnp.concatenate([grads[rows[first + s]] for s in range(slots)], axis=1)
            product = jnp.dot(lhs, rhs, preferred_element_type=F32)
            if len(refs) > 3:
                product += refs[0][k].astype(F32)
            out[k] = product.astype(BF)
        return 0

    lax.fori_loop(0, count // 2, step, 0)


def backward_part(adj, rows, cols, blocks, grads, arrived=None):
    slots, count = adj.shape[1], blocks.shape[0]
    smem, vmem = pl.BlockSpec(memory_space=pltpu.SMEM), pl.BlockSpec(memory_space=pltpu.VMEM)
    operands = [grads] if arrived is None else [grads, arrived]
    return pl.pallas_call(
        backward_kernel,
        in_specs=[smem] * 3 + [pl.BlockSpec(memory_space=pltpu.HBM)] + [vmem] * len(operands),
        out_specs=vmem,
        out_shape=jax.ShapeDtypeStruct((count, 256, 256), BF),
        scratch_shapes=[pltpu.VMEM((count, slots, 128, 128), BF), pltpu.SemaphoreType.DMA((count,))],
        cost_estimate=pl.CostEstimate(
            flops=2 * count * 768 * 256 * 256, bytes_accessed=count * (1 << 19) + (1 << 20), transcendentals=0
        ),
        compiler_params=pltpu.CompilerParams(vmem_limit_bytes=VMEM),
    )(blocks, rows, cols, adj, *operands)


def in_order(parts, position):
    count = len(parts)
    twice = jnp.stack(parts + parts[:-1])
    return lax.dynamic_slice_in_dim(twice, (count - position) % count, count, 0)


def scatter_sum(value, position, send):
    twice = jnp.concatenate([value, value[:3]], axis=0)
    mine = lax.dynamic_slice_in_dim(twice, position, 4, 0)
    total = mine[0]
    for d in (1, 3, 2):
        total = total + send(mine[d], d)
    return total


def gather(value, position, send):
    parts = [value, None, None, None]
    for d in (1, 3, 2):
        parts[d] = send(value, -d)
    return in_order(parts, position)


def sum_everywhere(value, core, x, y):
    halves = value.reshape(2, 320, 256)
    mine = jnp.where(core == 0, halves[0], halves[1])
    other = jnp.where(core == 0, halves[1], halves[0])
    part = mine + to_row(other, CORE)
    send_y = lambda v, d: to_col(v, ring_y(d))
    send_x = lambda v, d: lax.ppermute(v, ("row", "col"), ring_x(d))
    part = scatter_sum(part.reshape(4, 80, 256), y, send_y)
    part = scatter_sum(part.reshape(4, 20, 256), x, send_x)
    groups = [[(a * ZS + z) * 2 + c for z in range(ZS)] for a in range(2) for c in range(2)]
    every = lax.all_to_all(
        jnp.broadcast_to(part[None], (ZS,) + part.shape), "row", 0, 0, axis_index_groups=groups
    )
    part = jnp.sum(every, axis=0)
    part = gather(part, x, send_x).reshape(80, 256)
    part = gather(part, y, send_y).reshape(320, 256)
    other = to_row(part, CORE)
    low = jnp.where(core == 0, part, other)
    high = jnp.where(core == 0, other, part)
    return jnp.concatenate([low, high], axis=0)


def body(features, weight, adj_tiles, tile_row, tile_col, tile_count, train_mask, cotangent):
    row, col = lax.axis_index("row"), lax.axis_index("col")
    core, z, x_lo = row % 2, (row // 2) % ZS, row // 16
    y, x_hi = col // 2, col % 2
    adj = adj_tiles[0, 0]
    slots = adj.shape[1]
    live = jnp.arange(slots)[None, :] < tile_count[0, 0][:, None]
    cols = jnp.where(live, tile_col[0, 0], 2).reshape(-1)
    rows = tile_row[0, 0].reshape(-1)
    owner = rows // 2
    near = (((owner // 2 - y) % 4) * 2 + (owner % 2 ^ x_hi)) * 2 + rows % 2

    def block(d, far, across):
        return (x_lo ^ far) * 16 + ((z + d) % ZS) * 2 + (core ^ across)

    projected = jnp.dot(features, weight, preferred_element_type=F32).astype(BF)
    pair = jnp.stack([projected, to_row(projected, XLO)])

    def forward(arrived, total, last=False):
        pairs, blocks = [], []
        for d, both in arrived:
            pairs += [both, to_row(both, CORE)]
            blocks += [block(d, far, across) for across in (0, 1) for far in (0, 1)]
        return forward_part(adj, near, cols, jnp.stack(blocks), pairs, total, last)

    up, down = to_row(pair, ring_z(1)), to_row(pair, ring_z(-1))
    total = forward([(0, pair), (-1, up), (1, down)], None)
    up, down = to_row(up, ring_z(1)), to_row(down, ring_z(-1))
    second = [(-2, up), (2, down)]
    up, down = to_row(up, ring_z(1)), to_row(down, ring_z(-1))
    up, total = lax.optimization_barrier((up, total))
    third = [(-3, up), (3, down)]
    up = to_row(up, ring_z(1))
    total = forward(second, total)
    up, total = lax.optimization_barrier((up, total))
    parts = forward(third + [(4, up)], total, last=True)

    pre_act = parts[0]
    for d, far in ((2, 1), (2, 0), (1, 1), (1, 0), (3, 1), (3, 0), (0, 1)):
        route = [(i, (i + 2 * d) % COLS ^ far) for i in range(COLS)]
        pre_act = pre_act + to_col(parts[2 * d + far], route).astype(F32)
    gate = jax.nn.sigmoid(pre_act)
    hidden = (pre_act * gate).astype(BF)
    grad_pre = (
        cotangent.astype(F32) * train_mask.astype(F32)[:, None] * gate * (1.0 + pre_act * (1.0 - gate))
    ).astype(BF)

    mine = jnp.swapaxes(grad_pre.reshape(2, 128, 256), 1, 2)
    across_x = to_col(mine, XHI)
    pieces = [mine, across_x] + [None] * 6
    for d in (1, 3, 2):
        pieces[2 * d] = to_col(mine, ring_y(-d))
    for d in (1, 3, 2):
        pieces[2 * d + 1] = to_col(across_x, ring_y(-d))
    grads = jnp.concatenate(pieces, axis=0)

    order = [4, -3, 3, -2, 2, -1, 1, 0]
    blocks_of = lambda across: jnp.stack([block(d, far, across) for d in order for far in (0, 1)])
    mine, theirs = blocks_of(0), blocks_of(1)
    half = len(order)
    early = to_row(backward_part(adj, near, cols, theirs[:half], grads), CORE)
    late = to_row(backward_part(adj, near, cols, theirs[half:], grads), CORE)
    early = backward_part(adj, near, cols, mine[:half], grads, early)

    up, down = to_row(early[0:2], ring_z(1)), to_row(early[2:4], ring_z(-1))
    late = backward_part(adj, near, cols, mine[half:], grads, late)
    up, down, late = lax.optimization_barrier((up, down, late))

    def add(d, arrived):
        k = 2 * order.index(d)
        here = early[k : k + 2] if k < half else late[k - half : k - half + 2]
        return here.astype(F32) + arrived.astype(F32)

    up = to_row(add(3, up).astype(BF), ring_z(1))
    down = to_row(add(-2, down).astype(BF), ring_z(-1))
    features_t = features.T
    features_x = to_row(features_t, XLO)
    up = to_row(add(2, up).astype(BF), ring_z(1))
    down = to_row(add(-1, down).astype(BF), ring_z(-1))
    up = to_row(add(1, up).astype(BF), ring_z(1))
    both = add(0, up) + down.astype(F32)
    across_x = both[1].astype(BF)

    grad_scale = 1.0 / math.sqrt(ROWS * COLS * features.shape[0])
    local_grad = lax.dot_general(
        jnp.concatenate([features_t, features_x], axis=1),
        jnp.concatenate([both[0].astype(BF), across_x], axis=1),
        (((1,), (1,)), ((), ())),
        preferred_element_type=F32,
    )
    local_grad = jnp.pad(local_grad * grad_scale, ((0, WEIGHT_ROWS - features.shape[1]), (0, 0)))
    grad_proj = (both[0] + to_row(across_x, XLO).astype(F32)).astype(BF)
    grad_features = lax.dot_general(
        grad_proj, weight, (((0,), (1,)), ((), ())), preferred_element_type=F32
    ).astype(BF)
    grad_weight = sum_everywhere(local_grad, core, x_hi * 2 + x_lo, y)[: features.shape[1]]
    return (hidden, grad_features, grad_weight)


def solution(mesh):
    in_specs = (
        P(("row", "col"), None),
        P(),
        P("row", "col", None, None, None, None),
        P("row", "col", None, None),
        P("row", "col", None, None),
        P("row", "col", None),
        P(("row", "col")),
        P(("row", "col"), None),
    )
    out_specs = (P(("row", "col"), None), P(("row", "col"), None), P())
    return jax.shard_map(body, mesh=mesh, in_specs=in_specs, out_specs=out_specs, check_vma=False)
```

```python
import functools
import math

import jax
import jax.numpy as jnp
import numpy as np
from jax import lax
from jax.experimental import pallas as pl
from jax.experimental.pallas import tpu as pltpu
from jax.sharding import PartitionSpec as P

ROWS, COLS, ZS = 32, 8, 8
BF, F32 = jnp.bfloat16, jnp.float32
UP_DOWN = [0, -1, 1, -2, 2, -3, 3, 4]
FAR_FIRST = [4, -3, 3, -2, 2, -1, 1, 0]
VMEM = 60 << 20
WEIGHT_ROWS = 640

CORE = [(i, i ^ 1) for i in range(ROWS)]
XLO = [(i, i ^ 16) for i in range(ROWS)]
XHI = [(i, i ^ 1) for i in range(COLS)]


def ring_z(step):
    return [(i, (i // 16) * 16 + (i % 16 + 2 * step) % 16) for i in range(ROWS)]


def ring_y(step):
    return [(i, (i + 2 * step) % COLS) for i in range(COLS)]


def to_row(value, route):
    return lax.ppermute(value, "row", route)


def to_col(value, route):
    return lax.ppermute(value, "col", route)


def masked_tiles(tiles, cols, first):
    placed = []
    for s in range(tiles.shape[0]):
        tile, where = tiles[s], cols[first + s]
        zero = jnp.zeros_like(tile)
        placed.append(
            jnp.concatenate([jnp.where(where == 0, tile, zero), jnp.where(where == 1, tile, zero)], axis=1)
        )
    return jnp.concatenate(placed, axis=0)


def forward_kernel(base, half, fresh, last, blocks, rows, cols, adj, *refs):
    pairs, (held, tiles, total, held_sems, tile_sems, total_sem) = refs[:half], refs[-6:]
    outs = refs[half + (0 if fresh else 1) : -6]
    slots = tiles.shape[1]
    for q in range(half):
        if not last:
            pltpu.make_async_copy(pairs[q], held.at[q], held_sems.at[q]).start()
        for k in (2 * q, 2 * q + 1):
            pltpu.make_async_copy(adj.at[blocks[base + k]], tiles.at[k], tile_sems.at[k]).start()
    if fresh:
        total[...] = jnp.zeros_like(total)
    else:
        carried = pltpu.make_async_copy(refs[half], total, total_sem)
        carried.start()

    def step(q, _):
        if not last:
            pltpu.make_async_copy(pairs[0], held.at[q], held_sems.at[q]).wait()
        for k in (2 * q, 2 * q + 1):
            pltpu.make_async_copy(adj.at[0], tiles.at[k], tile_sems.at[k]).wait()
        products = []
        for far in range(2):
            k = 2 * q + far
            lhs = masked_tiles(tiles.at[k], cols, blocks[base + k] * slots)
            products.append(jnp.dot(lhs, pairs[q][far] if last else held[q, far], preferred_element_type=F32))
        if last and q == 0:
            carried.wait()
        for far in range(2):
            first = blocks[base + 2 * q + far] * slots
            for s in range(slots):
                total[rows[first + s]] += products[far][s * 128 : (s + 1) * 128]
        return 0

    if last:
        for q in range(half):
            step(q, 0)
    else:
        lax.fori_loop(0, half, step, 0)
        carried = pltpu.make_async_copy(total, outs[0], total_sem)
        carried.start()
        carried.wait()
        return
    outs[0][...] = total[:2].reshape(256, 256)
    for p in range(1, COLS):
        outs[p][...] = total[2 * p : 2 * p + 2].reshape(256, 256).astype(BF)


def forward_part(adj, rows, cols, blocks, base, pairs, total, last):
    slots, half = adj.shape[1], len(pairs)
    smem, hbm = pl.BlockSpec(memory_space=pltpu.SMEM), pl.BlockSpec(memory_space=pltpu.HBM)
    vmem = pl.BlockSpec(memory_space=pltpu.VMEM)
    operands = list(pairs) + ([] if total is None else [total])
    if last:
        shapes = [jax.ShapeDtypeStruct((256, 256), F32 if p == 0 else BF) for p in range(COLS)]
    else:
        shapes = [jax.ShapeDtypeStruct((16, 128, 256), F32)]
    outs = pl.pallas_call(
        functools.partial(forward_kernel, base, half, total is None, last),
        in_specs=[smem] * 3 + [hbm] + [vmem if last else hbm] * half + [hbm] * (len(operands) - half),
        out_specs=[vmem if last else hbm] * len(shapes),
        out_shape=shapes,
        scratch_shapes=[
            pltpu.VMEM((half, 2, 256, 256), BF),
            pltpu.VMEM((2 * half, slots, 128, 128), BF),
            pltpu.VMEM((16, 128, 256), F32),
            pltpu.SemaphoreType.DMA((half,)),
            pltpu.SemaphoreType.DMA((2 * half,)),
            pltpu.SemaphoreType.DMA,
        ],
        cost_estimate=pl.CostEstimate(
            flops=4 * half * 768 * 256 * 256, bytes_accessed=half * (1 << 20) + (1 << 22), transcendentals=0
        ),
        compiler_params=pltpu.CompilerParams(vmem_limit_bytes=VMEM),
    )(blocks, rows, cols, adj, *operands)
    return outs if last else outs[0]


def backward_kernel(base, blocks, rows, cols, adj, grads, out, tiles, sems):
    count, slots = tiles.shape[:2]
    for k in range(count):
        pltpu.make_async_copy(adj.at[blocks[base + k]], tiles.at[k], sems.at[k]).start()

    def step(q, _):
        for k in (2 * q, 2 * q + 1):
            pltpu.make_async_copy(adj.at[0], tiles.at[k], sems.at[k]).wait()
        for k in (2 * q, 2 * q + 1):
            first = blocks[base + k] * slots
            rhs = masked_tiles(tiles.at[k], cols, first)
            lhs = jnp.concatenate([grads[rows[first + s]] for s in range(slots)], axis=1)
            product = jnp.dot(lhs, rhs, preferred_element_type=F32)
            out[k] = product.astype(BF)
        return 0

    lax.fori_loop(0, count // 2, step, 0)


def backward_part(adj, rows, cols, blocks, base, count, grads):
    slots = adj.shape[1]
    smem, vmem = pl.BlockSpec(memory_space=pltpu.SMEM), pl.BlockSpec(memory_space=pltpu.VMEM)
    return pl.pallas_call(
        functools.partial(backward_kernel, base),
        in_specs=[smem] * 3 + [pl.BlockSpec(memory_space=pltpu.HBM)] + [vmem],
        out_specs=vmem,
        out_shape=jax.ShapeDtypeStruct((count, 256, 256), BF),
        scratch_shapes=[pltpu.VMEM((count, slots, 128, 128), BF), pltpu.SemaphoreType.DMA((count,))],
        cost_estimate=pl.CostEstimate(
            flops=2 * count * 768 * 256 * 256, bytes_accessed=count * (1 << 19) + (1 << 20), transcendentals=0
        ),
        compiler_params=pltpu.CompilerParams(vmem_limit_bytes=VMEM),
    )(blocks, rows, cols, adj, grads)


def sum_everywhere(value, core, beside):
    halves = value.reshape(2, 320, 256)
    mine = jnp.where(core == 0, halves[0], halves[1])
    other = jnp.where(core == 0, halves[1], halves[0])
    part = mine + to_row(other, CORE)
    part = jnp.sum(lax.all_to_all(part.reshape(COLS, 40, 256), "col", 0, 0), axis=0)
    part, beside = lax.optimization_barrier((part, beside))
    groups = [[2 * i + c for i in range(ROWS // 2)] for c in range(2)]
    every = jnp.broadcast_to(part.astype(BF)[None], (ROWS // 2,) + part.shape)
    every = lax.all_to_all(every, "row", 0, 0, axis_index_groups=groups)
    part = jnp.sum(every.astype(F32), axis=0)
    every = lax.all_to_all(jnp.broadcast_to(part[None], (COLS,) + part.shape), "col", 0, 0)
    part = every.reshape(320, 256)
    other = to_row(part, CORE)
    low = jnp.where(core == 0, part, other)
    high = jnp.where(core == 0, other, part)
    return jnp.concatenate([low, high], axis=0), beside


def body(features, weight, adj_tiles, tile_row, tile_col, tile_count, train_mask, cotangent):
    row, col = lax.axis_index("row"), lax.axis_index("col")
    core, z, x_lo = row % 2, (row // 2) % ZS, row // 16
    y, x_hi = col // 2, col % 2
    adj = adj_tiles[0, 0]
    slots = adj.shape[1]
    live = jnp.arange(slots)[None, :] < tile_count[0, 0][:, None]
    cols = jnp.where(live, tile_col[0, 0], 2).reshape(-1)
    rows = tile_row[0, 0].reshape(-1)
    owner = rows // 2
    near = (((owner // 2 - y) % 4) * 2 + (owner % 2 ^ x_hi)) * 2 + rows % 2

    forward_order = [(d, far, across) for d in UP_DOWN for across in (0, 1) for far in (0, 1)]
    backward_order = [(d, far, across) for across in (1, 0) for d in FAR_FIRST for far in (0, 1)]
    d, far, across = (jnp.asarray(v, jnp.int32) for v in np.array(forward_order + backward_order).T)
    blocks = (x_lo ^ far) * 16 + ((z + d) % ZS) * 2 + (core ^ across)

    projected = jnp.dot(features, weight, preferred_element_type=F32).astype(BF)
    pair = jnp.stack([projected, to_row(projected, XLO)])

    up = down = pair
    pairs = [pair, to_row(pair, CORE)]
    for k in range(1, 4):
        up, down = to_row(up, ring_z(1)), to_row(down, ring_z(-1))
        if k == 1:
            up, blocks, near, cols = lax.optimization_barrier((up, blocks, near, cols))
        pairs += [up, to_row(up, CORE), down, to_row(down, CORE)]
    up = to_row(up, ring_z(1))
    total = forward_part(adj, near, cols, blocks, 0, pairs, None, False)
    up, total = lax.optimization_barrier((up, total))
    parts = forward_part(adj, near, cols, blocks, 28, [up, to_row(up, CORE)], total, True)

    pre_act = parts[0]
    for d, far in ((2, 1), (2, 0), (1, 1), (1, 0), (3, 1), (3, 0), (0, 1)):
        route = [(i, (i + 2 * d) % COLS ^ far) for i in range(COLS)]
        pre_act = pre_act + to_col(parts[2 * d + far], route).astype(F32)
    gate = jax.nn.sigmoid(pre_act)
    hidden = (pre_act * gate).astype(BF)
    grad_pre = (
        cotangent.astype(F32) * train_mask.astype(F32)[:, None] * gate * (1.0 + pre_act * (1.0 - gate))
    ).astype(BF)

    mine = jnp.swapaxes(grad_pre.reshape(2, 128, 256), 1, 2)
    across_x = to_col(mine, XHI)
    pieces = [mine, across_x] + [None] * 6
    for d in (1, 3, 2):
        pieces[2 * d] = to_col(mine, ring_y(-d))
    for d in (1, 3, 2):
        pieces[2 * d + 1] = to_col(across_x, ring_y(-d))
    grads = jnp.concatenate(pieces, axis=0)

    theirs = backward_part(adj, near, cols, blocks, 32, 16, grads)
    theirs, grads = lax.optimization_barrier((theirs, grads))
    theirs = to_row(theirs, CORE)
    ours = backward_part(adj, near, cols, blocks, 48, 16, grads)

    def add(d, *arrived):
        k = 2 * FAR_FIRST.index(d)
        total = ours[k : k + 2].astype(F32) + theirs[k : k + 2].astype(F32)
        for value in arrived:
            total = total + value.astype(F32)
        return total

    up, down = lax.optimization_barrier((add(4).astype(BF), add(-3).astype(BF)))
    up, down = to_row(up, ring_z(1)), to_row(down, ring_z(-1))
    features_t = features.T
    for k in (3, 2, 1):
        up, down = add(k, up).astype(BF), (add(1 - k, down).astype(BF) if k > 1 else down)
        up, down = lax.optimization_barrier((up, down))
        up, down = to_row(up, ring_z(1)), (to_row(down, ring_z(-1)) if k > 1 else down)
        if k == 2:
            features_x = to_row(features_t, XLO)
    both = add(0, up, down)
    across_x = both[1].astype(BF)

    grad_scale = 1.0 / math.sqrt(ROWS * COLS * features.shape[0])
    local_grad = lax.dot_general(
        jnp.concatenate([features_t, features_x], axis=1),
        jnp.concatenate([both[0].astype(BF), across_x], axis=1),
        (((1,), (1,)), ((), ())),
        preferred_element_type=F32,
    )
    local_grad = jnp.pad(local_grad * grad_scale, ((0, WEIGHT_ROWS - features.shape[1]), (0, 0)))
    grad_proj = (both[0] + to_row(across_x, XLO).astype(F32)).astype(BF)
    grad_features = lax.dot_general(
        grad_proj, weight, (((0,), (1,)), ((), ())), preferred_element_type=F32
    ).astype(BF)
    grad_weight, grad_features = sum_everywhere(local_grad, core, grad_features)
    return (hidden, grad_features, grad_weight[: features.shape[1]])


def solution(mesh):
    in_specs = (
        P(("row", "col"), None),
        P(),
        P("row", "col", None, None, None, None),
        P("row", "col", None, None),
        P("row", "col", None, None),
        P("row", "col", None),
        P(("row", "col")),
        P(("row", "col"), None),
    )
    out_specs = (P(("row", "col"), None), P(("row", "col"), None), P())
    return jax.shard_map(body, mesh=mesh, in_specs=in_specs, out_specs=out_specs, check_vma=False)
```

```python
import functools
import math

import jax
import jax.numpy as jnp
import numpy as np
from jax import lax
from jax.experimental import pallas as pl
from jax.experimental.pallas import tpu as pltpu
from jax.sharding import PartitionSpec as P

ROWS, COLS, ZS = 32, 8, 8
BF, F32 = jnp.bfloat16, jnp.float32
UP_DOWN = [0, -1, 1, -2, 2, -3, 3, 4]
FAR_FIRST = [4, -3, 3, -2, 2, -1, 1, 0]
VMEM = 60 << 20
WEIGHT_ROWS = 640

CORE = [(i, i ^ 1) for i in range(ROWS)]
XLO = [(i, i ^ 16) for i in range(ROWS)]
XHI = [(i, i ^ 1) for i in range(COLS)]


def ring_z(step):
    return [(i, (i // 16) * 16 + (i % 16 + 2 * step) % 16) for i in range(ROWS)]


def ring_y(step):
    return [(i, (i + 2 * step) % COLS) for i in range(COLS)]


def to_row(value, route):
    return lax.ppermute(value, "row", route)


def to_col(value, route):
    return lax.ppermute(value, "col", route)


def masked_tiles(tiles, cols, first):
    placed = []
    for s in range(tiles.shape[0]):
        tile, where = tiles[s], cols[first + s]
        zero = jnp.zeros_like(tile)
        placed.append(
            jnp.concatenate([jnp.where(where == 0, tile, zero), jnp.where(where == 1, tile, zero)], axis=1)
        )
    return jnp.concatenate(placed, axis=0)


def forward_kernel(base, half, fresh, last, blocks, rows, cols, adj, *refs):
    pairs, (held, tiles, total, held_sems, tile_sems, total_sem) = refs[:half], refs[-6:]
    outs = refs[half + (0 if fresh else 1) : -6]
    slots = tiles.shape[1]
    for q in range(half):
        if not last:
            pltpu.make_async_copy(pairs[q], held.at[q], held_sems.at[q]).start()
        for k in (2 * q, 2 * q + 1):
            pltpu.make_async_copy(adj.at[blocks[base + k]], tiles.at[k], tile_sems.at[k]).start()
    if fresh:
        total[...] = jnp.zeros_like(total)
    else:
        carried = pltpu.make_async_copy(refs[half], total, total_sem)
        carried.start()

    def step(p, _):
        qs = [2 * p + i for i in range(2)]
        products = []
        for q in qs:
            if not last:
                pltpu.make_async_copy(pairs[0], held.at[q], held_sems.at[q]).wait()
            for k in (2 * q, 2 * q + 1):
                pltpu.make_async_copy(adj.at[0], tiles.at[k], tile_sems.at[k]).wait()
        for q in qs:
            for far in range(2):
                k = 2 * q + far
                lhs = masked_tiles(tiles.at[k], cols, blocks[base + k] * slots)
                rhs = pairs[q][far] if last else held[q, far]
                products.append((k, jnp.dot(lhs, rhs, preferred_element_type=F32)))
        if last:
            carried.wait()
        for k, product in products:
            first = blocks[base + k] * slots
            for s in range(slots):
                total[rows[first + s]] += product[s * 128 : (s + 1) * 128]
        return 0

    if last:
        step(0, 0)
    else:
        lax.fori_loop(0, half // 2, step, 0)
        carried = pltpu.make_async_copy(total, outs[0], total_sem)
        carried.start()
        carried.wait()
        return
    outs[0][...] = total[:2].reshape(256, 256)
    for p in range(1, COLS):
        outs[p][...] = total[2 * p : 2 * p + 2].reshape(256, 256).astype(BF)


def forward_part(adj, rows, cols, blocks, base, pairs, total, last):
    slots, half = adj.shape[1], len(pairs)
    smem, hbm = pl.BlockSpec(memory_space=pltpu.SMEM), pl.BlockSpec(memory_space=pltpu.HBM)
    vmem = pl.BlockSpec(memory_space=pltpu.VMEM)
    operands = list(pairs) + ([] if total is None else [total])
    if last:
        shapes = [jax.ShapeDtypeStruct((256, 256), F32 if p == 0 else BF) for p in range(COLS)]
    else:
        shapes = [jax.ShapeDtypeStruct((16, 128, 256), F32)]
    outs = pl.pallas_call(
        functools.partial(forward_kernel, base, half, total is None, last),
        in_specs=[smem] * 3 + [hbm] + [vmem if last else hbm] * half + [hbm] * (len(operands) - half),
        out_specs=[vmem if last else hbm] * len(shapes),
        out_shape=shapes,
        scratch_shapes=[
            pltpu.VMEM((half, 2, 256, 256), BF),
            pltpu.VMEM((2 * half, slots, 128, 128), BF),
            pltpu.VMEM((16, 128, 256), F32),
            pltpu.SemaphoreType.DMA((half,)),
            pltpu.SemaphoreType.DMA((2 * half,)),
            pltpu.SemaphoreType.DMA,
        ],
        cost_estimate=pl.CostEstimate(
            flops=4 * half * 768 * 256 * 256, bytes_accessed=half * (1 << 20) + (1 << 22), transcendentals=0
        ),
        compiler_params=pltpu.CompilerParams(vmem_limit_bytes=VMEM),
    )(blocks, rows, cols, adj, *operands)
    return outs if last else outs[0]


def backward_kernel(base, blocks, rows, cols, adj, *refs):
    pieces, (out, held, tiles, results, held_sems, tile_sems, out_sems) = refs[:COLS], refs[COLS:]
    count, slots = tiles.shape[:2]
    arrivals = [
        pltpu.make_async_copy(pieces[p], held.at[pl.ds(2 * p, 2)], held_sems.at[p]) for p in range(COLS)
    ]
    for arrival in arrivals:
        arrival.start()
    for k in range(count):
        pltpu.make_async_copy(adj.at[blocks[base + k]], tiles.at[k], tile_sems.at[k]).start()
    for arrival in arrivals:
        arrival.wait()

    def step(q, _):
        ks = [8 * q + i for i in range(8)]
        for k in ks:
            pltpu.make_async_copy(adj.at[0], tiles.at[k], tile_sems.at[k]).wait()
        for k in ks:
            first = blocks[base + k] * slots
            rhs = masked_tiles(tiles.at[k], cols, first)
            lhs = jnp.concatenate([held[rows[first + s]] for s in range(slots)], axis=1)
            results[k] = jnp.dot(lhs, rhs, preferred_element_type=F32).astype(BF)
        for k in ks:
            pltpu.make_async_copy(results.at[k], out.at[k], out_sems.at[k]).start()
        return 0

    lax.fori_loop(0, count // 8, step, 0)
    for k in range(count):
        pltpu.make_async_copy(results.at[k], out.at[k], out_sems.at[k]).wait()


def backward_part(adj, rows, cols, blocks, base, count, grads):
    slots = adj.shape[1]
    smem, hbm = pl.BlockSpec(memory_space=pltpu.SMEM), pl.BlockSpec(memory_space=pltpu.HBM)
    return pl.pallas_call(
        functools.partial(backward_kernel, base),
        in_specs=[smem] * 3 + [hbm] * (1 + COLS),
        out_specs=hbm,
        out_shape=jax.ShapeDtypeStruct((count, 256, 256), BF),
        scratch_shapes=[
            pltpu.VMEM((16, 256, 128), BF),
            pltpu.VMEM((count, slots, 128, 128), BF),
            pltpu.VMEM((count, 256, 256), BF),
            pltpu.SemaphoreType.DMA((COLS,)),
            pltpu.SemaphoreType.DMA((count,)),
            pltpu.SemaphoreType.DMA((count,)),
        ],
        cost_estimate=pl.CostEstimate(
            flops=2 * count * 768 * 256 * 256, bytes_accessed=count * (1 << 19) + (1 << 20), transcendentals=0
        ),
        compiler_params=pltpu.CompilerParams(vmem_limit_bytes=VMEM),
    )(blocks, rows, cols, adj, *grads)


def sum_everywhere(value, core, beside):
    halves = value.reshape(2, 320, 256)
    mine = jnp.where(core == 0, halves[0], halves[1])
    other = jnp.where(core == 0, halves[1], halves[0])
    part = mine + to_row(other, CORE)
    part = jnp.sum(lax.all_to_all(part.reshape(COLS, 40, 256), "col", 0, 0), axis=0)
    part, beside = lax.optimization_barrier((part, beside))
    groups = [[2 * i + c for i in range(ROWS // 2)] for c in range(2)]
    every = jnp.broadcast_to(part.astype(BF)[None], (ROWS // 2,) + part.shape)
    every = lax.all_to_all(every, "row", 0, 0, axis_index_groups=groups)
    part = jnp.sum(every.astype(F32), axis=0)
    every = lax.all_to_all(jnp.broadcast_to(part[None], (COLS,) + part.shape), "col", 0, 0)
    part = every.reshape(320, 256)
    other = to_row(part, CORE)
    low = jnp.where(core == 0, part, other)
    high = jnp.where(core == 0, other, part)
    return jnp.concatenate([low, high], axis=0), beside


def body(features, weight, adj_tiles, tile_row, tile_col, tile_count, train_mask, cotangent):
    row, col = lax.axis_index("row"), lax.axis_index("col")
    core, z, x_lo = row % 2, (row // 2) % ZS, row // 16
    y, x_hi = col // 2, col % 2
    adj = adj_tiles[0, 0]
    slots = adj.shape[1]
    live = jnp.arange(slots)[None, :] < tile_count[0, 0][:, None]
    cols = jnp.where(live, tile_col[0, 0], 2).reshape(-1)
    rows = tile_row[0, 0].reshape(-1)
    owner = rows // 2
    near = (((owner // 2 - y) % 4) * 2 + (owner % 2 ^ x_hi)) * 2 + rows % 2

    forward_order = [(d, far, across) for d in UP_DOWN for across in (0, 1) for far in (0, 1)]
    backward_order = [(d, far, across) for across in (1, 0) for d in FAR_FIRST for far in (0, 1)]
    d, far, across = (jnp.asarray(v, jnp.int32) for v in np.array(forward_order + backward_order).T)
    blocks = (x_lo ^ far) * 16 + ((z + d) % ZS) * 2 + (core ^ across)

    projected = jnp.dot(features, weight, preferred_element_type=F32).astype(BF)
    pair = jnp.stack([projected, to_row(projected, XLO)])

    up = down = pair
    pairs = [pair, to_row(pair, CORE)]
    for k in range(1, 4):
        up, down = to_row(up, ring_z(1)), to_row(down, ring_z(-1))
        if k == 1:
            up, blocks, near, cols = lax.optimization_barrier((up, blocks, near, cols))
        pairs += [up, to_row(up, CORE), down, to_row(down, CORE)]
    up = to_row(up, ring_z(1))
    total = forward_part(adj, near, cols, blocks, 0, pairs, None, False)
    up, total = lax.optimization_barrier((up, total))
    parts = forward_part(adj, near, cols, blocks, 28, [up, to_row(up, CORE)], total, True)

    pre_act = parts[0]
    for d, far in ((2, 1), (2, 0), (1, 1), (1, 0), (3, 1), (3, 0), (0, 1)):
        route = [(i, (i + 2 * d) % COLS ^ far) for i in range(COLS)]
        pre_act = pre_act + to_col(parts[2 * d + far], route).astype(F32)
    gate = jax.nn.sigmoid(pre_act)
    hidden = (pre_act * gate).astype(BF)
    grad_pre = (
        cotangent.astype(F32) * train_mask.astype(F32)[:, None] * gate * (1.0 + pre_act * (1.0 - gate))
    ).astype(BF)

    mine = jnp.swapaxes(grad_pre.reshape(2, 128, 256), 1, 2)
    across_x = to_col(mine, XHI)
    pieces = [mine, across_x] + [None] * 6
    for d in (1, 3, 2):
        pieces[2 * d] = to_col(mine, ring_y(-d))
    for d in (1, 3, 2):
        pieces[2 * d + 1] = to_col(across_x, ring_y(-d))
    grads = pieces

    theirs = backward_part(adj, near, cols, blocks, 32, 16, grads)
    theirs, grads = lax.optimization_barrier((theirs, grads))
    theirs = to_row(theirs, CORE)
    ours = backward_part(adj, near, cols, blocks, 48, 16, grads)

    def add(d, *arrived):
        k = 2 * FAR_FIRST.index(d)
        total = ours[k : k + 2].astype(F32) + theirs[k : k + 2].astype(F32)
        for value in arrived:
            total = total + value.astype(F32)
        return total

    up, down = lax.optimization_barrier((add(4).astype(BF), add(-3).astype(BF)))
    up, down = to_row(up, ring_z(1)), to_row(down, ring_z(-1))
    features_t = features.T
    for k in (3, 2, 1):
        here_up, here_down = add(k), (add(1 - k) if k > 1 else add(0))
        up, down, here_up, here_down = lax.optimization_barrier((up, down, here_up, here_down))
        up = (here_up + up.astype(F32)).astype(BF)
        if k > 1:
            down = (here_down + down.astype(F32)).astype(BF)
            up, down = lax.optimization_barrier((up, down))
            down = to_row(down, ring_z(-1))
        up = to_row(up, ring_z(1))
        if k == 2:
            features_x = to_row(features_t, XLO)
    both = here_down + up.astype(F32) + down.astype(F32)
    across_x = both[1].astype(BF)

    grad_scale = 1.0 / math.sqrt(ROWS * COLS * features.shape[0])
    local_grad = lax.dot_general(
        jnp.concatenate([features_t, features_x], axis=1),
        jnp.concatenate([both[0].astype(BF), across_x], axis=1),
        (((1,), (1,)), ((), ())),
        preferred_element_type=F32,
    )
    local_grad = jnp.pad(local_grad * grad_scale, ((0, WEIGHT_ROWS - features.shape[1]), (0, 0)))
    grad_proj = (both[0] + to_row(across_x, XLO).astype(F32)).astype(BF)
    grad_features = lax.dot_general(
        grad_proj, weight, (((0,), (1,)), ((), ())), preferred_element_type=F32
    ).astype(BF)
    grad_weight, grad_features = sum_everywhere(local_grad, core, grad_features)
    return (hidden, grad_features, grad_weight[: features.shape[1]])


def solution(mesh):
    in_specs = (
        P(("row", "col"), None),
        P(),
        P("row", "col", None, None, None, None),
        P("row", "col", None, None),
        P("row", "col", None, None),
        P("row", "col", None),
        P(("row", "col")),
        P(("row", "col"), None),
    )
    out_specs = (P(("row", "col"), None), P(("row", "col"), None), P())
    return jax.shard_map(body, mesh=mesh, in_specs=in_specs, out_specs=out_specs, check_vma=False)
```

```python
import functools
import math

import jax
import jax.numpy as jnp
import numpy as np
from jax import lax
from jax.experimental import pallas as pl
from jax.experimental.pallas import tpu as pltpu
from jax.sharding import PartitionSpec as P

ROWS, COLS, ZS = 32, 8, 8
BF, F32 = jnp.bfloat16, jnp.float32
UP_DOWN = [0, -1, 1, -2, 2, -3, 3, 4]
FAR_FIRST = [4, -3, 3, -2, 2, -1, 1, 0]
VMEM = 60 << 20
WEIGHT_ROWS = 640

CORE = [(i, i ^ 1) for i in range(ROWS)]
XLO = [(i, i ^ 16) for i in range(ROWS)]
XHI = [(i, i ^ 1) for i in range(COLS)]


def ring_z(step):
    return [(i, (i // 16) * 16 + (i % 16 + 2 * step) % 16) for i in range(ROWS)]


def ring_y(step):
    return [(i, (i + 2 * step) % COLS) for i in range(COLS)]


def to_row(value, route):
    return lax.ppermute(value, "row", route)


def to_col(value, route):
    return lax.ppermute(value, "col", route)


def masked_tiles(tiles, cols, first):
    placed = []
    for s in range(tiles.shape[0]):
        tile, where = tiles[s], cols[first + s]
        zero = jnp.zeros_like(tile)
        placed.append(
            jnp.concatenate([jnp.where(where == 0, tile, zero), jnp.where(where == 1, tile, zero)], axis=1)
        )
    return jnp.concatenate(placed, axis=0)


def forward_kernel(base, half, fresh, last, blocks, rows, cols, adj, *refs):
    pairs, (held, tiles, total, held_sems, tile_sems, total_sem) = refs[:half], refs[-6:]
    outs = refs[half + (0 if fresh else 1) : -6]
    slots = tiles.shape[1]
    for q in range(half):
        if not last:
            pltpu.make_async_copy(pairs[q], held.at[q], held_sems.at[q]).start()
        for k in (2 * q, 2 * q + 1):
            pltpu.make_async_copy(adj.at[blocks[base + k]], tiles.at[k], tile_sems.at[k]).start()
    if fresh:
        total[...] = jnp.zeros_like(total)
    else:
        carried = pltpu.make_async_copy(refs[half], total, total_sem)
        carried.start()

    def step(p, _):
        qs = [2 * p + i for i in range(2)]
        products = []
        for q in qs:
            if not last:
                pltpu.make_async_copy(pairs[0], held.at[q], held_sems.at[q]).wait()
            for k in (2 * q, 2 * q + 1):
                pltpu.make_async_copy(adj.at[0], tiles.at[k], tile_sems.at[k]).wait()
        for q in qs:
            for far in range(2):
                k = 2 * q + far
                lhs = masked_tiles(tiles.at[k], cols, blocks[base + k] * slots)
                rhs = pairs[q][far] if last else held[q, far]
                products.append((k, jnp.dot(lhs, rhs, preferred_element_type=F32)))
        if last:
            carried.wait()
        for k, product in products:
            first = blocks[base + k] * slots
            for s in range(slots):
                total[rows[first + s]] += product[s * 128 : (s + 1) * 128]
        return 0

    if last:
        step(0, 0)
    else:
        lax.fori_loop(0, half // 2, step, 0)
        carried = pltpu.make_async_copy(total, outs[0], total_sem)
        carried.start()
        carried.wait()
        return
    outs[0][...] = total[:2].reshape(256, 256)
    for p in range(1, COLS):
        outs[p][...] = total[2 * p : 2 * p + 2].reshape(256, 256).astype(BF)


def forward_part(adj, rows, cols, blocks, base, pairs, total, last):
    slots, half = adj.shape[1], len(pairs)
    smem, hbm = pl.BlockSpec(memory_space=pltpu.SMEM), pl.BlockSpec(memory_space=pltpu.HBM)
    vmem = pl.BlockSpec(memory_space=pltpu.VMEM)
    operands = list(pairs) + ([] if total is None else [total])
    if last:
        shapes = [jax.ShapeDtypeStruct((256, 256), F32 if p == 0 else BF) for p in range(COLS)]
    else:
        shapes = [jax.ShapeDtypeStruct((16, 128, 256), F32)]
    outs = pl.pallas_call(
        functools.partial(forward_kernel, base, half, total is None, last),
        in_specs=[smem] * 3 + [hbm] + [vmem if last else hbm] * half + [hbm] * (len(operands) - half),
        out_specs=[vmem if last else hbm] * len(shapes),
        out_shape=shapes,
        scratch_shapes=[
            pltpu.VMEM((half, 2, 256, 256), BF),
            pltpu.VMEM((2 * half, slots, 128, 128), BF),
            pltpu.VMEM((16, 128, 256), F32),
            pltpu.SemaphoreType.DMA((half,)),
            pltpu.SemaphoreType.DMA((2 * half,)),
            pltpu.SemaphoreType.DMA,
        ],
        cost_estimate=pl.CostEstimate(
            flops=4 * half * 768 * 256 * 256, bytes_accessed=half * (1 << 20) + (1 << 22), transcendentals=0
        ),
        compiler_params=pltpu.CompilerParams(vmem_limit_bytes=VMEM),
    )(blocks, rows, cols, adj, *operands)
    return outs if last else outs[0]


def backward_kernel(base, blocks, rows, cols, adj, *refs):
    pieces, (out, held, tiles, results, held_sems, tile_sems, out_sems) = refs[:COLS], refs[COLS:]
    count, slots = tiles.shape[:2]
    group = 8 if count % 8 == 0 else 4
    arrivals = [
        pltpu.make_async_copy(pieces[p], held.at[pl.ds(2 * p, 2)], held_sems.at[p]) for p in range(COLS)
    ]
    for arrival in arrivals:
        arrival.start()
    for k in range(count):
        pltpu.make_async_copy(adj.at[blocks[base + k]], tiles.at[k], tile_sems.at[k]).start()
    for arrival in arrivals:
        arrival.wait()

    def step(q, _):
        ks = [group * q + i for i in range(group)]
        for k in ks:
            pltpu.make_async_copy(adj.at[0], tiles.at[k], tile_sems.at[k]).wait()
        for k in ks:
            first = blocks[base + k] * slots
            rhs = masked_tiles(tiles.at[k], cols, first)
            lhs = jnp.concatenate([held[rows[first + s]] for s in range(slots)], axis=1)
            results[k] = jnp.dot(lhs, rhs, preferred_element_type=F32).astype(BF)
        for k in ks:
            pltpu.make_async_copy(results.at[k], out.at[k], out_sems.at[k]).start()
        return 0

    lax.fori_loop(0, count // group, step, 0)
    for k in range(count):
        pltpu.make_async_copy(results.at[k], out.at[k], out_sems.at[k]).wait()


def backward_part(adj, rows, cols, blocks, base, count, grads):
    slots = adj.shape[1]
    smem, hbm = pl.BlockSpec(memory_space=pltpu.SMEM), pl.BlockSpec(memory_space=pltpu.HBM)
    return pl.pallas_call(
        functools.partial(backward_kernel, base),
        in_specs=[smem] * 3 + [hbm] * (1 + COLS),
        out_specs=hbm,
        out_shape=jax.ShapeDtypeStruct((count, 256, 256), BF),
        scratch_shapes=[
            pltpu.VMEM((16, 256, 128), BF),
            pltpu.VMEM((count, slots, 128, 128), BF),
            pltpu.VMEM((count, 256, 256), BF),
            pltpu.SemaphoreType.DMA((COLS,)),
            pltpu.SemaphoreType.DMA((count,)),
            pltpu.SemaphoreType.DMA((count,)),
        ],
        cost_estimate=pl.CostEstimate(
            flops=2 * count * 768 * 256 * 256, bytes_accessed=count * (1 << 19) + (1 << 20), transcendentals=0
        ),
        compiler_params=pltpu.CompilerParams(vmem_limit_bytes=VMEM),
    )(blocks, rows, cols, adj, *grads)


def sum_everywhere(value, core, beside):
    halves = value.reshape(2, 320, 256)
    mine = jnp.where(core == 0, halves[0], halves[1])
    other = jnp.where(core == 0, halves[1], halves[0])
    part = mine + to_row(other, CORE)
    parts = lax.all_to_all(part.astype(BF).reshape(COLS, 40, 256), "col", 0, 0)
    part = jnp.sum(parts.astype(F32), axis=0)
    part, beside = lax.optimization_barrier((part, beside))
    groups = [[2 * i + c for i in range(ROWS // 2)] for c in range(2)]
    every = jnp.broadcast_to(part.astype(BF)[None], (ROWS // 2,) + part.shape)
    every = lax.all_to_all(every, "row", 0, 0, axis_index_groups=groups)
    part = jnp.sum(every.astype(F32), axis=0)
    every = lax.all_to_all(jnp.broadcast_to(part[None], (COLS,) + part.shape), "col", 0, 0)
    part = every.reshape(320, 256)
    other = to_row(part, CORE)
    low = jnp.where(core == 0, part, other)
    high = jnp.where(core == 0, other, part)
    return jnp.concatenate([low, high], axis=0), beside


def body(features, weight, adj_tiles, tile_row, tile_col, tile_count, train_mask, cotangent):
    row, col = lax.axis_index("row"), lax.axis_index("col")
    core, z, x_lo = row % 2, (row // 2) % ZS, row // 16
    y, x_hi = col // 2, col % 2
    adj = adj_tiles[0, 0]
    slots = adj.shape[1]
    live = jnp.arange(slots)[None, :] < tile_count[0, 0][:, None]
    cols = jnp.where(live, tile_col[0, 0], 2).reshape(-1)
    rows = tile_row[0, 0].reshape(-1)
    owner = rows // 2
    near = (((owner // 2 - y) % 4) * 2 + (owner % 2 ^ x_hi)) * 2 + rows % 2

    forward_order = [(d, far, across) for d in UP_DOWN for across in (0, 1) for far in (0, 1)]
    backward_order = [(d, far, across) for across in (1, 0) for d in FAR_FIRST for far in (0, 1)]
    d, far, across = (jnp.asarray(v, jnp.int32) for v in np.array(forward_order + backward_order).T)
    blocks = (x_lo ^ far) * 16 + ((z + d) % ZS) * 2 + (core ^ across)

    projected = jnp.dot(features, weight, preferred_element_type=F32).astype(BF)
    pair = jnp.stack([projected, to_row(projected, XLO)])

    up = down = pair
    pairs = [pair, to_row(pair, CORE)]
    for k in range(1, 4):
        up, down = to_row(up, ring_z(1)), to_row(down, ring_z(-1))
        if k == 1:
            up, blocks, near, cols = lax.optimization_barrier((up, blocks, near, cols))
        pairs += [up, to_row(up, CORE), down, to_row(down, CORE)]
    up = to_row(up, ring_z(1))
    total = forward_part(adj, near, cols, blocks, 0, pairs, None, False)
    up, total = lax.optimization_barrier((up, total))
    parts = forward_part(adj, near, cols, blocks, 28, [up, to_row(up, CORE)], total, True)

    pre_act = parts[0]
    for d, far in ((0, 1), (1, 0), (3, 0), (2, 0), (1, 1), (3, 1), (2, 1)):
        route = [(i, (i + 2 * d) % COLS ^ far) for i in range(COLS)]
        pre_act = pre_act + to_col(parts[2 * d + far], route).astype(F32)
    gate = jax.nn.sigmoid(pre_act)
    hidden = (pre_act * gate).astype(BF)
    grad_pre = (
        cotangent.astype(F32) * train_mask.astype(F32)[:, None] * gate * (1.0 + pre_act * (1.0 - gate))
    ).astype(BF)

    mine = jnp.swapaxes(grad_pre.reshape(2, 128, 256), 1, 2)
    across_x = to_col(mine, XHI)
    pieces = [mine, across_x] + [None] * 6
    for d in (1, 3, 2):
        pieces[2 * d] = to_col(mine, ring_y(-d))
    for d in (1, 3, 2):
        pieces[2 * d + 1] = to_col(across_x, ring_y(-d))
    grads = pieces

    theirs = backward_part(adj, near, cols, blocks, 32, 16, grads)
    theirs, grads = lax.optimization_barrier((theirs, grads))
    theirs = to_row(theirs, CORE)
    first = backward_part(adj, near, cols, blocks, 48, 4, grads)

    sums = (first.astype(F32) + theirs[:4].astype(F32)).astype(BF)
    up, down, grads = lax.optimization_barrier((sums[:2], sums[2:], grads))
    up, down = to_row(up, ring_z(1)), to_row(down, ring_z(-1))
    rest = backward_part(adj, near, cols, blocks, 52, 12, grads)

    def add(d):
        k = 2 * FAR_FIRST.index(d)
        return rest[k - 4 : k - 2].astype(F32) + theirs[k : k + 2].astype(F32)

    features_t = features.T
    for k in (3, 2, 1):
        here_up, here_down = add(k), (add(1 - k) if k > 1 else add(0))
        up, down, here_up, here_down = lax.optimization_barrier((up, down, here_up, here_down))
        up = (here_up + up.astype(F32)).astype(BF)
        if k > 1:
            down = (here_down + down.astype(F32)).astype(BF)
            up, down = lax.optimization_barrier((up, down))
            down = to_row(down, ring_z(-1))
        up = to_row(up, ring_z(1))
        if k == 2:
            features_x = to_row(features_t, XLO)
    both = here_down + up.astype(F32) + down.astype(F32)
    across_x = both[1].astype(BF)

    grad_scale = 1.0 / math.sqrt(ROWS * COLS * features.shape[0])
    local_grad = lax.dot_general(
        jnp.concatenate([features_t, features_x], axis=1),
        jnp.concatenate([both[0].astype(BF), across_x], axis=1),
        (((1,), (1,)), ((), ())),
        preferred_element_type=F32,
    )
    local_grad = jnp.pad(local_grad * grad_scale, ((0, WEIGHT_ROWS - features.shape[1]), (0, 0)))
    grad_proj = (both[0] + to_row(across_x, XLO).astype(F32)).astype(BF)
    grad_features = lax.dot_general(
        grad_proj, weight, (((0,), (1,)), ((), ())), preferred_element_type=F32
    ).astype(BF)
    grad_weight, grad_features = sum_everywhere(local_grad, core, grad_features)
    return (hidden, grad_features, grad_weight[: features.shape[1]])


def solution(mesh):
    in_specs = (
        P(("row", "col"), None),
        P(),
        P("row", "col", None, None, None, None),
        P("row", "col", None, None),
        P("row", "col", None, None),
        P("row", "col", None),
        P(("row", "col")),
        P(("row", "col"), None),
    )
    out_specs = (P(("row", "col"), None), P(("row", "col"), None), P())
    return jax.shard_map(body, mesh=mesh, in_specs=in_specs, out_specs=out_specs, check_vma=False)
```
